32 devices in a mesh: gx: 4 (over y, x), gy: 4 (over z), gz: 2 (over core).
Axes of the slice: x: 2, y: 2, z: 4, core: 2. Of those that a mesh axis runs over, the one named last changes fastest.
Arguments:
- orbitals: float32 [4, 256, 256, 256], P(None, 'gx', 'gy', 'gz'), may hold values from -6 to 6
- potential: float32 [256, 256, 256], P('gx', 'gy', 'gz'), may hold values from -2 to 0
Outputs:
- basis: float32 [4, 256, 256, 256], P(None, 'gx', 'gy', 'gz')
- factor: float32 [4, 4], replicated
The draws below stay inside these ranges and needn't reach their ends.
All inputs are finite; a program needn't handle non-finite values.
Results may differ from the reference program's by a relative error of at most 0.00011.
Values sent between devices are 32-bit elements; how exact they have to be, the bound alone decides.
No kernel may reach another device: no remote copies, remote signals or barrier semaphores. Data moves between devices by JAX's collectives and lax.ppermute only.
A program may use at most 256 MiB of HBM per device.

```python
import jax
import jax.numpy as jnp
from jax import lax

NORB = 4
NX = 256
NY = 256
NZ = 256


def shard_levels(own_key, shape, shards, least, largest):
    gain, own = 1.0, jax.random.fold_in(own_key, 6)
    for position, blocks in shards:
        steps = jnp.exp(jax.random.uniform(jax.random.fold_in(own, position), (blocks,), jnp.float32, least / len(shards), largest / len(shards)))
        gain = gain * jnp.repeat(steps, shape[position] // blocks).reshape([-1 if axis == position else 1 for axis in range(len(shape))])
    return gain


def bell_draw(key, shape, scale, bound, cuts=(), kind=jnp.bfloat16):
    values = scale * jax.random.normal(key, shape, jnp.float32)
    if cuts:
        values = values * shard_levels(key, shape, cuts, -0.22, 0.18)
    return jnp.clip(values, -bound, bound).astype(kind)


def setup_inputs(seed: int = 0) -> dict:
    keys = jax.random.split(jax.random.key(seed), 3)
    orbitals = bell_draw(keys[0], (NORB, NX, NY, NZ), 1.0, 6.0, ((1, 4), (2, 4), (3, 2)), jnp.float32)
    potential = jnp.clip(-2.0 + 2.0 * jax.random.uniform(keys[1], (NX, NY, NZ), jnp.float32) ** shard_levels(keys[1], (NX, NY, NZ), ((0, 4), (1, 4), (2, 2)), -0.2, 0.2), -2.0, 0.0)
    return {"orbitals": orbitals, "potential": potential}


def shifted(padded, axis, offset):
    pieces = []
    for which in range(3):
        length = padded.shape[which - 3]
        if which - 3 == axis:
            pieces.append(slice(2 + offset, length - 2 + offset))
        else:
            pieces.append(slice(2, length - 2))
    return padded[..., pieces[0], pieces[1], pieces[2]]

def kinetic(padded):
    total = -7.5 * shifted(padded, -1, 0)
    for axis in (-3, -2, -1):
        for offset, weight in ((1, 4.0 / 3.0), (2, -1.0 / 12.0)):
            total = total + weight * (shifted(padded, axis, offset) + shifted(padded, axis, -offset))
    return -0.5 * total

def apply_hamiltonian(field, potential):
    padded = jnp.pad(field, ((0, 0), (2, 2), (2, 2), (2, 2)))
    return kinetic(padded) + potential[None] * field

def reference(orbitals, potential):
    centre = 4.5
    half_width = 3.5
    level_zero = orbitals
    level_one = (apply_hamiltonian(level_zero, potential) - centre * level_zero) / half_width
    level_two = 2.0 * (apply_hamiltonian(level_one, potential) - centre * level_one) / half_width - level_zero
    filtered = 2.0 * (apply_hamiltonian(level_two, potential) - centre * level_two) / half_width - level_one
    gram = jnp.einsum('iabc,jabc->ij', filtered, filtered, precision=lax.Precision.HIGHEST) / (NX * NY * NZ)
    factor = jnp.linalg.cholesky(gram).T
    inverse = jax.scipy.linalg.solve_triangular(factor, jnp.eye(NORB, dtype=factor.dtype), lower=False)
    basis = jnp.einsum('ij,iabc->jabc', inverse, filtered, precision=lax.Precision.HIGHEST)
    return (basis, factor)
```

```python
import functools

import jax
import jax.numpy as jnp
from jax import lax
from jax.experimental import pallas as pl
from jax.experimental.pallas import tpu as pltpu
from jax.sharding import PartitionSpec as P

CENTRE = 4.5
HALF_WIDTH = 3.5
SCALE = 2.0 / HALF_WIDTH
EDGE = SCALE / 24.0
LANES = 128
TILE = 8
PAD = 8
VMEM_LIMIT = 8 * 1024 * 1024


def vmem_out(shape):
    return pltpu.VMEM(shape, jnp.float32)


def in_vmem(array):
    return pltpu.with_memory_space_constraint(array, pltpu.VMEM)


WHOLE = pl.BlockSpec(memory_space=pltpu.VMEM)
ANYWHERE = pl.BlockSpec(memory_space=pl.ANY)


def params():
    return pltpu.CompilerParams(vmem_limit_bytes=VMEM_LIMIT)


def cost(flops, moved):
    return pl.CostEstimate(flops=flops, bytes_accessed=moved, transcendentals=0)


def pairing(axis, parity):
    pairs = []
    for low in range(parity, lax.axis_size(axis) - 1, 2):
        pairs += [(low, low + 1), (low + 1, low)]
    return pairs


def swap(array, axis, parity):
    pairs = pairing(axis, parity)
    if not pairs:
        return jnp.zeros_like(array)
    return lax.ppermute(array, axis, pairs)


def is_odd(axis):
    return lax.rem(lax.axis_index(axis), 2) == 1


def faces_x_kernel(field, even, odd, sems):
    count = field.shape[1]
    low = field.at[:, pl.ds(0, 2)]
    high = field.at[:, pl.ds(count - 2, 2)]
    flip = is_odd("gx")

    def move(first, second):
        one = pltpu.make_async_copy(first, even, sems.at[0])
        two = pltpu.make_async_copy(second, odd, sems.at[1])
        one.start()
        two.start()
        one.wait()
        two.wait()

    @pl.when(flip)
    def _():
        move(low, high)

    @pl.when(jnp.logical_not(flip))
    def _():
        move(high, low)


def faces_x(orbitals):
    orbs, _, ny, nz = orbitals.shape
    shape = vmem_out((orbs, 2, ny, nz))
    return pl.pallas_call(
        faces_x_kernel,
        out_shape=(shape, shape),
        in_specs=[ANYWHERE],
        out_specs=(WHOLE, WHOLE),
        scratch_shapes=[pltpu.SemaphoreType.DMA((2,))],
        compiler_params=params(),
        name="faces_x",
    )(orbitals)


def pack_y_group(rows, even, odd, orb, group, flip):
    place = pl.ds(group * TILE, TILE)
    for layer in range(2):
        low, high = rows[layer], rows[2 + layer]
        even[orb, layer, place, :] = jnp.where(flip, low, high)
        odd[orb, layer, place, :] = jnp.where(flip, high, low)


def load_kernel(nx, ny, field, potential, out, weight, even, odd, sems):
    orbs = field.shape[0]
    pitch = ny + PAD
    flat = out.reshape(orbs, (nx + 4) * pitch, LANES)
    copies = []
    for orb in range(orbs):
        copy = pltpu.make_async_copy(
            field.at[orb], out.at[orb, pl.ds(2, nx), pl.ds(0, ny)], sems.at[orb]
        )
        copy.start()
        copies.append(copy)
    flip = is_odd("gy")
    zero_planes = jnp.zeros((2 * pitch, LANES), jnp.float32)
    zero_rows = jnp.zeros((PAD, LANES), jnp.float32)
    for orb in range(orbs):
        flat[orb, pl.ds(0, 2 * pitch), :] = zero_planes
        flat[orb, pl.ds((nx + 2) * pitch, 2 * pitch), :] = zero_planes

        @pl.loop(0, nx, unroll=8)
        def _(x):
            flat[orb, pl.ds(pl.multiple_of((x + 2) * pitch + ny, TILE), PAD), :] = zero_rows

    @pl.loop(0, nx, unroll=2)
    def _(x):
        weight[x] = SCALE * potential[x] + SCALE * (0.5 * 7.5 - CENTRE)

    for orb in range(orbs):
        copies[orb].wait()

        @pl.loop(0, nx // TILE, unroll=2)
        def _(group):
            start = (group * TILE + 2) * pitch
            rows = [
                flat[orb, pl.ds(start + y, TILE, stride=pitch), :] for y in (0, 1, ny - 2, ny - 1)
            ]
            pack_y_group(rows, even, odd, orb, group, flip)


def load(orbitals, potential):
    orbs, nx, ny, nz = orbitals.shape
    face = vmem_out((orbs, 2, nx, nz))
    return pl.pallas_call(
        functools.partial(load_kernel, nx, ny),
        out_shape=(
            vmem_out((orbs, nx + 4, ny + PAD, nz)),
            vmem_out((nx, ny, nz)),
            face,
            face,
        ),
        in_specs=[ANYWHERE, WHOLE],
        out_specs=(WHOLE,) * 4,
        scratch_shapes=[pltpu.SemaphoreType.DMA((orbs,))],
        compiler_params=params(),
        cost_estimate=cost(0, orbitals.size * 8),
        name="load",
    )(orbitals, potential)


def pack_z_kernel(nx, ny, field, packed):
    orbs = field.shape[0]
    pitch = ny + PAD
    per = LANES // 4
    lane = lax.broadcasted_iota(jnp.int32, (TILE, LANES), 1)
    flat = field.reshape(orbs, (nx + 4) * pitch, LANES)
    unroll = 8

    @pl.loop(0, orbs * (nx // per))
    def _(index):
        orb = index // (nx // per)
        group = index % (nx // per)

        @pl.loop(0, ny // TILE)
        def _(tile):
            def step(part, total):
                for which in range(unroll):
                    plane = part * unroll + which
                    start = pl.multiple_of(
                        (group * per + plane + 2) * pitch + tile * TILE, TILE
                    )
                    rows = flat[orb, pl.ds(start, TILE), :]
                    moved = pltpu.roll(rows, 4 * which + 2, 1)
                    total = jnp.where(lane // 4 == which, moved, total)
                return pltpu.roll(total, LANES - 4 * unroll, 1)

            total = jnp.zeros((TILE, LANES), jnp.float32)
            for part in range(per // unroll):
                total = step(part, total)
            packed[orb, group, pl.ds(pl.multiple_of(tile * TILE, TILE), TILE), :] = total


def pack_z(field, nx, ny):
    orbs = field.shape[0]
    return pl.pallas_call(
        functools.partial(pack_z_kernel, nx, ny),
        out_shape=vmem_out((orbs, nx * 4 // LANES, ny, LANES)),
        in_specs=[WHOLE],
        out_specs=WHOLE,
        compiler_params=params(),
        cost_estimate=cost(0, field.size * 4),
        name="pack_z",
    )(in_vmem(field))


def step_kernel(nx, ny, first, field, weight, own, z_even, z_odd, *rest):
    if first:
        out, correction = rest
    else:
        before, out, correction = rest
    orbs = field.shape[0]
    pitch = ny + PAD
    per = LANES // 4
    flat = field.reshape(orbs, (nx + 4) * pitch, LANES)
    flat_out = out.reshape(orbs, (nx + 4) * pitch, LANES)
    edge = EDGE * (0.5 if first else 1.0)
    chunk = 8
    flip = is_odd("gz")
    wide = lax.broadcasted_iota(jnp.int32, (ny, LANES), 1) % 4
    lane = lax.broadcasted_iota(jnp.int32, (TILE, LANES), 1)
    ends = (lane < 2) | (lane >= LANES - 2)

    if first:
        zero_planes = jnp.zeros((2 * pitch, LANES), jnp.float32)
        zero_rows = jnp.zeros((PAD, LANES), jnp.float32)
        for orb in range(orbs):
            flat_out[orb, pl.ds(0, 2 * pitch), :] = zero_planes
            flat_out[orb, pl.ds((nx + 2) * pitch, 2 * pitch), :] = zero_planes

            @pl.loop(0, nx, unroll=8)
            def _(x):
                place = pl.ds(pl.multiple_of((x + 2) * pitch + ny, TILE), PAD)
                flat_out[orb, place, :] = zero_rows

    for orb in range(orbs):
        for group in range(nx // per):
            mine = own[orb, group]
            even, odd = z_even[orb, group], z_odd[orb, group]
            below = jnp.where(flip, even, odd)
            above = jnp.where(flip, odd, even)
            gap = jnp.where(wide < 2, below, above) - mine
            left = pltpu.roll(gap, LANES - 2, 1) - 16.0 * jnp.where(
                wide == 1, pltpu.roll(gap, LANES - 1, 1), 0.0
            )
            right = pltpu.roll(gap, 2, 1) - 16.0 * jnp.where(
                wide == 2, pltpu.roll(gap, 1, 1), 0.0
            )
            correction[orb, group] = edge * jnp.where(wide < 2, left, right)

    @pl.loop(0, orbs)
    def _(orb):
        @pl.loop(0, nx // chunk)
        def _(part):
            x0 = part * chunk
            group = x0 // per
            turn = lax.rem(LANES - 4 * lax.rem(x0, per), LANES)

            for tile in range(ny // TILE):
                base = (x0 + 2) * pitch + tile * TILE

                def rows(plane, shift=0):
                    start = base + plane * pitch + shift
                    if shift == 0:
                        start = pl.multiple_of(start, TILE)
                    return flat[orb, pl.ds(start, TILE), :]

                mine = [rows(plane) for plane in range(-2, chunk + 2)]
                place = pl.ds(tile * TILE, TILE)
                fix = pltpu.roll(correction[orb, group, place, :], turn, 1)
                for plane in range(chunk):
                    centre = mine[plane + 2]
                    near = (
                        (mine[plane + 1] + mine[plane + 3])
                        + (rows(plane, -1) + rows(plane, 1))
                        + (pltpu.roll(centre, 1, 1) + pltpu.roll(centre, LANES - 1, 1))
                    )
                    far = (
                        (mine[plane] + mine[plane + 4])
                        + (rows(plane, -2) + rows(plane, 2))
                        + (pltpu.roll(centre, 2, 1) + pltpu.roll(centre, LANES - 2, 1))
                    )
                    ours = weight[x0 + plane, place, :]
                    if first:
                        ours = 0.5 * ours
                    value = ours * centre + edge * (far - 16.0 * near)
                    value = value + jnp.where(
                        ends, pltpu.roll(fix, LANES - 4 * plane - 2, 1), 0.0
                    )
                    there = pl.ds(pl.multiple_of(base + plane * pitch, TILE), TILE)
                    if not first:
                        value = value - flat_before(before, orbs, nx, pitch)[orb, there, :]
                    flat_out[orb, there, :] = value


def flat_before(before, orbs, nx, pitch):
    return before.reshape(orbs, (nx + 4) * pitch, LANES)


def step(field, weight, packed, z_even, z_odd, before):
    orbs = field.shape[0]
    nx, ny, nz = weight.shape
    first = before is None
    args = [field, weight, packed, z_even, z_odd] + ([] if first else [before])
    return pl.pallas_call(
        functools.partial(step_kernel, nx, ny, first),
        out_shape=vmem_out(field.shape),
        in_specs=[WHOLE] * len(args),
        out_specs=WHOLE,
        scratch_shapes=[pltpu.VMEM(packed.shape, jnp.float32)],
        input_output_aliases={} if first else {5: 0},
        compiler_params=params(),
        cost_estimate=cost(field.size * 20, field.size * 12),
        name="step",
    )(*[in_vmem(arg) for arg in args])


def edges_kernel(nx, ny, edge, last, field, x_even, x_odd, y_even, y_odd, out, *faces):
    orbs = field.shape[0]
    pitch = ny + PAD
    flat = out.reshape(orbs, (nx + 4) * pitch, LANES)
    flip_x, flip_y = is_odd("gx"), is_odd("gy")
    if not last:
        next_x_even, next_x_odd, next_y_even, next_y_odd = faces

    def plane_rows(x):
        return pl.ds((x + 2) * pitch, ny)

    @pl.loop(0, orbs)
    def _(orb):
        def halves(layer):
            even, odd = x_even[orb, layer], x_odd[orb, layer]
            return jnp.where(flip_x, even, odd), jnp.where(flip_x, odd, even)

        low_far, high_near = halves(0)
        low_near, high_far = halves(1)
        flat[orb, plane_rows(0), :] += edge * (low_far - 16.0 * low_near)
        flat[orb, plane_rows(1), :] += edge * low_near
        flat[orb, plane_rows(nx - 2), :] += edge * high_near
        flat[orb, plane_rows(nx - 1), :] += edge * (high_far - 16.0 * high_near)

        @pl.loop(0, nx // TILE, unroll=2)
        def _(group):
            place = pl.ds(group * TILE, TILE)

            def pick(layer):
                even, odd = y_even[orb, layer, place, :], y_odd[orb, layer, place, :]
                return jnp.where(flip_y, even, odd), jnp.where(flip_y, odd, even)

            low_far, high_near = pick(0)
            low_near, high_far = pick(1)
            adds = (
                edge * (low_far - 16.0 * low_near),
                edge * low_near,
                edge * high_near,
                edge * (high_far - 16.0 * high_near),
            )
            start = (group * TILE + 2) * pitch
            rows = []
            for y, add in zip((0, 1, ny - 2, ny - 1), adds):
                there = pl.ds(start + y, TILE, stride=pitch)
                value = flat[orb, there, :] + add
                flat[orb, there, :] = value
                rows.append(value)
            if not last:
                pack_y_group(rows, next_y_even, next_y_odd, orb, group, flip_y)

        if not last:
            for layer in range(2):
                low = flat[orb, plane_rows(layer), :]
                high = flat[orb, plane_rows(nx - 2 + layer), :]
                next_x_even[orb, layer] = jnp.where(flip_x, low, high)
                next_x_odd[orb, layer] = jnp.where(flip_x, high, low)


def edges(field, nx, ny, halos, edge, last):
    orbs, nz = field.shape[0], field.shape[-1]
    shapes = [vmem_out(field.shape)]
    if not last:
        shapes += [vmem_out((orbs, 2, ny, nz))] * 2 + [vmem_out((orbs, 2, nx, nz))] * 2
    return pl.pallas_call(
        functools.partial(edges_kernel, nx, ny, edge, last),
        out_shape=tuple(shapes),
        in_specs=[WHOLE] * 5,
        out_specs=(WHOLE,) * len(shapes),
        input_output_aliases={0: 0},
        compiler_params=params(),
        cost_estimate=cost(0, field.size),
        name="edges",
    )(*[in_vmem(arg) for arg in (field, *halos)])


PAIRS = [(line, column) for line in range(4) for column in range(line, 4)]


def pair_list(orbs):
    return [(line, column) for line in range(orbs) for column in range(line, orbs)]


def gram_kernel(nx, ny, field, out):
    orbs = field.shape[0]
    pitch = ny + PAD
    flat = field.reshape(orbs, (nx + 4) * pitch, LANES)
    pairs = pair_list(orbs)

    def plane(x, totals):
        totals = list(totals)
        for tile in range(ny // TILE):
            start = pl.multiple_of((x + 2) * pitch + tile * TILE, TILE)
            rows = [flat[orb, pl.ds(start, TILE), :] for orb in range(orbs)]
            for index, (line, column) in enumerate(pairs):
                totals[index] = totals[index] + rows[line] * rows[column]
        return tuple(totals)

    zero = jnp.zeros((TILE, LANES), jnp.float32)
    totals = lax.fori_loop(0, nx, plane, (zero,) * len(pairs))
    out[...] = jnp.zeros_like(out)
    for index, total in enumerate(totals):
        out[pl.ds(index, 1), :] = jnp.sum(total, axis=0, keepdims=True)


def gram(field, nx, ny):
    orbs = field.shape[0]
    rows = -(-len(pair_list(orbs)) // TILE) * TILE
    return pl.pallas_call(
        functools.partial(gram_kernel, nx, ny),
        out_shape=jax.ShapeDtypeStruct((rows, LANES), jnp.float32),
        in_specs=[WHOLE],
        out_specs=WHOLE,
        compiler_params=params(),
        name="gram",
    )(in_vmem(field))


def basis_kernel(nx, ny, chunk, cells, parts, field, *rest):
    sums, (out, factor, inverse) = rest[:parts], rest[parts:]
    orbs = field.shape[0]
    pitch = ny + PAD
    flat = field.reshape(orbs, (nx + 4) * pitch, LANES)
    pairs = pair_list(orbs)

    @pl.when(pl.program_id(0) == 0)
    def _():
        total = sums[0][...]
        for part in sums[1:]:
            total = total + part[...]
        total = jnp.broadcast_to(jnp.sum(total, axis=1, keepdims=True), total.shape) / cells
        entry = {}
        for index, pair in enumerate(pairs):
            entry[pair] = total[index : index + 1, :]
        upper, inv = {}, {}
        for line in range(orbs):
            for column in range(line, orbs):
                value = entry[line, column]
                for inner in range(line):
                    value = value - upper[inner, line] * upper[inner, column]
                if column == line:
                    upper[line, line] = jnp.sqrt(value)
                    inv[line, line] = 1.0 / upper[line, line]
                else:
                    upper[line, column] = value * inv[line, line]
        for column in range(orbs):
            for line in range(column - 1, -1, -1):
                value = upper[line, line + 1] * inv[line + 1, column]
                for inner in range(line + 2, column + 1):
                    value = value + upper[line, inner] * inv[inner, column]
                inv[line, column] = -value * inv[line, line]
        row = lax.broadcasted_iota(jnp.int32, (TILE, LANES), 0)
        col = lax.broadcasted_iota(jnp.int32, (TILE, LANES), 1)
        whole = jnp.zeros((TILE, LANES), jnp.float32)
        for (line, column), value in upper.items():
            there = (row == line) & (col == column)
            whole = jnp.where(there, jnp.broadcast_to(value, whole.shape), whole)
        factor[...] = whole[:orbs, :orbs]
        for index, pair in enumerate(pairs):
            inverse[index] = jnp.broadcast_to(inv[pair], (TILE, LANES))

    first = pl.program_id(0) * chunk
    gains = {pair: inverse[index] for index, pair in enumerate(pairs)}

    @pl.loop(0, chunk)
    def _(plane):
        for tile in range(ny // TILE):
            start = pl.multiple_of((first + plane + 2) * pitch + tile * TILE, TILE)
            rows = [flat[orb, pl.ds(start, TILE), :] for orb in range(orbs)]
            for column in range(orbs):
                value = rows[0] * gains[0, column]
                for line in range(1, column + 1):
                    value = value + rows[line] * gains[line, column]
                out[column, plane, pl.ds(tile * TILE, TILE), :] = value


def basis(field, nx, ny, sums, cells):
    orbs, nz = field.shape[0], field.shape[-1]
    chunk = 4
    return pl.pallas_call(
        functools.partial(basis_kernel, nx, ny, chunk, cells, len(sums)),
        out_shape=(
            jax.ShapeDtypeStruct((orbs, nx, ny, nz), jnp.float32),
            jax.ShapeDtypeStruct((orbs, orbs), jnp.float32),
        ),
        grid=(nx // chunk,),
        in_specs=[WHOLE] * (1 + len(sums)),
        out_specs=(
            pl.BlockSpec((orbs, chunk, ny, nz), lambda i: (0, i, 0, 0)),
            pl.BlockSpec((orbs, orbs), lambda i: (0, 0)),
        ),
        scratch_shapes=[pltpu.VMEM((len(pair_list(orbs)), TILE, LANES), jnp.float32)],
        compiler_params=params(),
        name="basis",
    )(in_vmem(field), *sums)


def rotations(array, axis):
    count = lax.axis_size(axis)
    return [
        lax.ppermute(array, axis, [(i, (i + by) % count) for i in range(count)])
        for by in range(1, count)
    ]


def body(orbitals, potential):
    _, nx, ny, _ = orbitals.shape
    cells = (
        nx
        * lax.axis_size("gx")
        * (ny * lax.axis_size("gy"))
        * (orbitals.shape[3] * lax.axis_size("gz"))
    )
    x_faces = faces_x(orbitals)
    halo_x = [swap(face, "gx", parity) for parity, face in enumerate(x_faces)]
    field, weight, *y_faces = load(orbitals, potential)
    before = None
    for level in range(3):
        last = level == 2
        halo_y = [swap(face, "gy", parity) for parity, face in enumerate(y_faces)]
        packed = pack_z(field, nx, ny)
        z_even, z_odd = swap(packed, "gz", 0), swap(packed, "gz", 1)
        after = step(field, weight, packed, z_even, z_odd, before)
        edge = EDGE * (0.5 if level == 0 else 1.0)
        after, *faces = edges(after, nx, ny, (*halo_x, *halo_y), edge, last)
        if not last:
            halo_x = [swap(face, "gx", parity) for parity, face in enumerate(faces[:2])]
            y_faces = faces[2:]
        before, field = field, after
    local = gram(field, nx, ny)
    for axis in ("gz", "gy"):
        for part in rotations(local, axis):
            local = local + part
    return basis(field, nx, ny, [local, *rotations(local, "gx")], cells)


def solution(mesh):
    return jax.shard_map(
        body,
        mesh=mesh,
        in_specs=(P(None, "gx", "gy", "gz"), P("gx", "gy", "gz")),
        out_specs=(P(None, "gx", "gy", "gz"), P()),
        check_vma=False,
    )
```

```python
import functools

import jax
import jax.numpy as jnp
from jax import lax
from jax.experimental import pallas as pl
from jax.experimental.pallas import tpu as pltpu
from jax.sharding import PartitionSpec as P

CENTRE = 4.5
HALF_WIDTH = 3.5
SCALE = 2.0 / HALF_WIDTH
EDGE = SCALE / 24.0
LANES = 128
TILE = 8
PAD = 8
PER = LANES // 4
VMEM_LIMIT = 8 * 1024 * 1024


def vmem_out(shape):
    return pltpu.VMEM(shape, jnp.float32)


def in_vmem(array):
    return pltpu.with_memory_space_constraint(array, pltpu.VMEM)


WHOLE = pl.BlockSpec(memory_space=pltpu.VMEM)
ANYWHERE = pl.BlockSpec(memory_space=pl.ANY)


def params():
    return pltpu.CompilerParams(vmem_limit_bytes=VMEM_LIMIT)


LITTLE = pl.CostEstimate(flops=1, bytes_accessed=1, transcendentals=0)


def pairing(axis, parity):
    pairs = []
    for low in range(parity, lax.axis_size(axis) - 1, 2):
        pairs += [(low, low + 1), (low + 1, low)]
    return pairs


def swap(array, axis, parity):
    pairs = pairing(axis, parity)
    if not pairs:
        return jnp.zeros_like(array)
    return lax.ppermute(array, axis, pairs)


def is_odd(axis):
    return lax.rem(lax.axis_index(axis), 2) == 1


def faces_x_kernel(field, even, odd, sems):
    count = field.shape[1]
    low = field.at[:, pl.ds(0, 2)]
    high = field.at[:, pl.ds(count - 2, 2)]
    flip = is_odd("gx")

    def move(first, second):
        one = pltpu.make_async_copy(first, even, sems.at[0])
        two = pltpu.make_async_copy(second, odd, sems.at[1])
        one.start()
        two.start()
        one.wait()
        two.wait()

    @pl.when(flip)
    def _():
        move(low, high)

    @pl.when(jnp.logical_not(flip))
    def _():
        move(high, low)


def faces_x(orbitals):
    orbs, _, ny, nz = orbitals.shape
    shape = vmem_out((orbs, 2, ny, nz))
    return pl.pallas_call(
        faces_x_kernel,
        out_shape=(shape, shape),
        in_specs=[ANYWHERE],
        out_specs=(WHOLE, WHOLE),
        scratch_shapes=[pltpu.SemaphoreType.DMA((2,))],
        compiler_params=params(),
        cost_estimate=LITTLE,
        name="faces_x",
    )(orbitals)


def pack_y_group(rows, even, odd, orb, group, flip):
    place = pl.ds(group * TILE, TILE)
    for layer in range(2):
        low, high = rows[layer], rows[2 + layer]
        even[orb, layer, place, :] = jnp.where(flip, low, high)
        odd[orb, layer, place, :] = jnp.where(flip, high, low)


def pack_z_lanes(rows, plane, total):
    lane = lax.broadcasted_iota(jnp.int32, rows.shape, 1)
    moved = pltpu.roll(rows, (4 * plane + 2) % LANES, 1)
    return moved if total is None else jnp.where(lane // 4 == plane, moved, total)


def pack_z_tiles(flat, packed, pitch, orb, group, tiles):
    totals = [None] * len(tiles)
    for plane in range(PER):
        for number, tile in enumerate(tiles):
            start = pl.multiple_of((group * PER + plane + 2) * pitch + tile * TILE, TILE)
            rows = flat[orb, pl.ds(start, TILE), :]
            totals[number] = pack_z_lanes(rows, plane, totals[number])
    for number, tile in enumerate(tiles):
        packed[orb, group, pl.ds(tile * TILE, TILE), :] = totals[number]


def load_kernel(nx, ny, field, potential, out, weight, even, odd, packed, sems):
    orbs = field.shape[0]
    pitch = ny + PAD
    flat = out.reshape(orbs, (nx + 4) * pitch, LANES)
    copies = []
    for orb in range(orbs):
        copy = pltpu.make_async_copy(
            field.at[orb], out.at[orb, pl.ds(2, nx), pl.ds(0, ny)], sems.at[orb]
        )
        copy.start()
        copies.append(copy)
    last = pltpu.make_async_copy(potential, weight, sems.at[orbs])
    last.start()
    flip = is_odd("gy")
    zero_planes = jnp.zeros((2 * pitch, LANES), jnp.float32)
    zero_rows = jnp.zeros((PAD, LANES), jnp.float32)
    for orb in range(orbs):
        flat[orb, pl.ds(0, 2 * pitch), :] = zero_planes
        flat[orb, pl.ds((nx + 2) * pitch, 2 * pitch), :] = zero_planes

        @pl.loop(0, nx, unroll=8)
        def _(x):
            flat[orb, pl.ds(pl.multiple_of((x + 2) * pitch + ny, TILE), PAD), :] = zero_rows

    for orb in range(orbs):
        copies[orb].wait()

        @pl.loop(0, nx // TILE, unroll=2)
        def _(group):
            start = (group * TILE + 2) * pitch
            rows = [
                flat[orb, pl.ds(start + y, TILE, stride=pitch), :] for y in (0, 1, ny - 2, ny - 1)
            ]
            pack_y_group(rows, even, odd, orb, group, flip)

        @pl.loop(0, nx // PER)
        def _(group):
            pack_z_tiles(flat, packed, pitch, orb, group, range(ny // TILE))

    last.wait()

    @pl.loop(0, nx, unroll=2)
    def _(x):
        weight[x] = SCALE * weight[x] + SCALE * (0.5 * 7.5 - CENTRE)


def load(orbitals, potential):
    orbs, nx, ny, nz = orbitals.shape
    face = vmem_out((orbs, 2, nx, nz))
    return pl.pallas_call(
        functools.partial(load_kernel, nx, ny),
        out_shape=(
            vmem_out((orbs, nx + 4, ny + PAD, nz)),
            vmem_out((nx, ny, nz)),
            face,
            face,
            vmem_out((orbs, nx // PER, ny, nz)),
        ),
        in_specs=[ANYWHERE, ANYWHERE],
        out_specs=(WHOLE,) * 5,
        scratch_shapes=[pltpu.SemaphoreType.DMA((orbs + 1,))],
        compiler_params=params(),
        cost_estimate=LITTLE,
        name="load",
    )(orbitals, potential)


def step_kernel(nx, ny, first, last, field, weight, z_even, z_odd, *rest):
    rest = rest if first else rest[1:]
    out, packed = rest[0], None if last else rest[1]
    correction, mix = rest[-2:]
    orbs = field.shape[0]
    pitch = ny + PAD
    flat = field.reshape(orbs, (nx + 4) * pitch, LANES)
    flat_out = out.reshape(orbs, (nx + 4) * pitch, LANES)
    edge = EDGE * (0.5 if first else 1.0)
    groups = nx // PER
    tiles = ny // TILE
    flip = is_odd("gz")
    place = lax.broadcasted_iota(jnp.int32, (ny, LANES), 1) % 4
    lane = lax.broadcasted_iota(jnp.int32, (TILE, LANES), 1)
    ends = (lane < 2) | (lane >= LANES - 2)

    if first:
        zero_planes = jnp.zeros((2 * pitch, LANES), jnp.float32)
        zero_rows = jnp.zeros((PAD, LANES), jnp.float32)
        for orb in range(orbs):
            flat_out[orb, pl.ds(0, 2 * pitch), :] = zero_planes
            flat_out[orb, pl.ds((nx + 2) * pitch, 2 * pitch), :] = zero_planes

            @pl.loop(0, nx, unroll=8)
            def _(x):
                there = pl.ds(pl.multiple_of((x + 2) * pitch + ny, TILE), PAD)
                flat_out[orb, there, :] = zero_rows

    line = lax.broadcasted_iota(jnp.int32, (LANES, LANES), 0)
    column = lax.broadcasted_iota(jnp.int32, (LANES, LANES), 1)
    apart = jnp.abs(line - column)
    weights = jnp.where(apart == 1, -16.0, jnp.where(apart == 2, 1.0, 0.0)).astype(jnp.bfloat16)
    mix[pl.ds(0, LANES), :] = weights
    mix[pl.ds(LANES, LANES), :] = weights

    for orb in range(orbs):
        for group in range(groups):
            even, odd = z_even[orb, group], z_odd[orb, group]
            below = jnp.where(flip, even, odd)
            above = jnp.where(flip, odd, even)
            beyond = jnp.where(place < 2, below, above)
            left = pltpu.roll(beyond, LANES - 2, 1) - 16.0 * jnp.where(
                place == 1, pltpu.roll(beyond, LANES - 1, 1), 0.0
            )
            right = pltpu.roll(beyond, 2, 1) - 16.0 * jnp.where(
                place == 2, pltpu.roll(beyond, 1, 1), 0.0
            )
            correction[orb, group] = jnp.where(place < 2, left, right)

    def locate(index, tile):
        orb, group = index // groups, lax.rem(index, groups)
        return orb, group, (group * PER + 2) * pitch + tile * TILE

    def along_z(index, tile):
        orb, group, base = locate(index, tile)
        rows = [
            flat[orb, pl.ds(pl.multiple_of(base + plane * pitch, TILE), TILE), :]
            for plane in range(PER)
        ]
        stacked = jnp.concatenate(rows, axis=0)
        high = stacked.astype(jnp.bfloat16)
        low = (stacked - high.astype(jnp.float32)).astype(jnp.bfloat16)
        product = jnp.dot(
            jnp.concatenate([high, low], axis=1), mix[...], preferred_element_type=jnp.float32
        )
        fix = correction[orb, group, pl.ds(tile * TILE, TILE), :]
        sums = []
        for plane in range(PER):
            moved = pltpu.roll(fix, LANES - 4 * plane - 2, 1)
            sums.append(
                product[plane * TILE : (plane + 1) * TILE] + jnp.where(ends, moved, 0.0)
            )
        return tuple(sums)

    def block(index, sums):
        for tile in range(tiles):
            if tile + 1 < tiles:
                later = along_z(index, tile + 1)
            else:
                later = along_z(jnp.minimum(index + 1, orbs * groups - 1), 0)
            finish(index, tile, sums)
            sums = later
        return sums

    def finish(index, tile, sums):
        orb, group, base = locate(index, tile)

        def rows(plane, shift=0):
            start = base + plane * pitch + shift
            if shift == 0:
                start = pl.multiple_of(start, TILE)
            return flat[orb, pl.ds(start, TILE), :]

        mine = [rows(plane) for plane in range(-2, PER + 2)]
        values = []
        total = None
        for plane in range(PER):
            near = (mine[plane + 1] + mine[plane + 3]) + (rows(plane, -1) + rows(plane, 1))
            far = (mine[plane] + mine[plane + 4]) + (rows(plane, -2) + rows(plane, 2))
            ours = weight[group * PER + plane, pl.ds(tile * TILE, TILE), :]
            if first:
                ours = 0.5 * ours
            value = ours * mine[plane + 2] + edge * ((far - 16.0 * near) + sums[plane])
            if not first:
                start = pl.multiple_of(base + plane * pitch, TILE)
                value = value - flat_out[orb, pl.ds(start, TILE), :]
            if not last:
                total = pack_z_lanes(value, plane, total)
            values.append(value)
        for plane in range(PER):
            start = pl.multiple_of(base + plane * pitch, TILE)
            flat_out[orb, pl.ds(start, TILE), :] = values[plane]
        if not last:
            packed[orb, group, pl.ds(tile * TILE, TILE), :] = total

    lax.fori_loop(0, orbs * groups, block, along_z(0, 0))


def step(field, weight, z_even, z_odd, before, last):
    orbs = field.shape[0]
    nx, ny, nz = weight.shape
    first = before is None
    args = [field, weight, z_even, z_odd] + ([] if first else [before])
    shapes = [vmem_out(field.shape)] + ([] if last else [vmem_out(z_even.shape)])
    return pl.pallas_call(
        functools.partial(step_kernel, nx, ny, first, last),
        out_shape=tuple(shapes),
        in_specs=[WHOLE] * len(args),
        out_specs=(WHOLE,) * len(shapes),
        scratch_shapes=[
            pltpu.VMEM((orbs, nx // PER, ny, nz), jnp.float32),
            pltpu.VMEM((2 * nz, nz), jnp.bfloat16),
        ],
        input_output_aliases={} if first else {4: 0},
        compiler_params=params(),
        cost_estimate=LITTLE,
        name="step",
    )(*[in_vmem(arg) for arg in args])


def edges_kernel(nx, ny, edge, last, field, x_even, x_odd, y_even, y_odd, *rest):
    orbs = field.shape[0]
    pitch = ny + PAD
    if last:
        (out,) = rest
    else:
        _, out, next_x_even, next_x_odd, next_y_even, next_y_odd, packed = rest
    flat = out.reshape(orbs, (nx + 4) * pitch, LANES)
    flip_x, flip_y = is_odd("gx"), is_odd("gy")

    def plane_rows(x):
        return pl.ds((x + 2) * pitch, ny)

    @pl.loop(0, orbs)
    def _(orb):
        def halves(layer):
            even, odd = x_even[orb, layer], x_odd[orb, layer]
            return jnp.where(flip_x, even, odd), jnp.where(flip_x, odd, even)

        low_far, high_near = halves(0)
        low_near, high_far = halves(1)
        flat[orb, plane_rows(0), :] += edge * (low_far - 16.0 * low_near)
        flat[orb, plane_rows(1), :] += edge * low_near
        flat[orb, plane_rows(nx - 2), :] += edge * high_near
        flat[orb, plane_rows(nx - 1), :] += edge * (high_far - 16.0 * high_near)

        @pl.loop(0, nx // TILE, unroll=2)
        def _(group):
            place = pl.ds(group * TILE, TILE)

            def pick(layer):
                even, odd = y_even[orb, layer, place, :], y_odd[orb, layer, place, :]
                return jnp.where(flip_y, even, odd), jnp.where(flip_y, odd, even)

            low_far, high_near = pick(0)
            low_near, high_far = pick(1)
            adds = (
                edge * (low_far - 16.0 * low_near),
                edge * low_near,
                edge * high_near,
                edge * (high_far - 16.0 * high_near),
            )
            start = (group * TILE + 2) * pitch
            rows = []
            for y, add in zip((0, 1, ny - 2, ny - 1), adds):
                there = pl.ds(start + y, TILE, stride=pitch)
                value = flat[orb, there, :] + add
                flat[orb, there, :] = value
                rows.append(value)
            if not last:
                pack_y_group(rows, next_y_even, next_y_odd, orb, group, flip_y)

        if not last:
            for layer in range(2):
                low = flat[orb, plane_rows(layer), :]
                high = flat[orb, plane_rows(nx - 2 + layer), :]
                next_x_even[orb, layer] = jnp.where(flip_x, low, high)
                next_x_odd[orb, layer] = jnp.where(flip_x, high, low)

            tiles = ny // TILE
            for group in range(nx // PER):
                pack_z_tiles(flat, packed, pitch, orb, group, (0, tiles - 1))
            for x in (0, 1, nx - 2, nx - 1):
                group, plane = x // PER, x % PER
                there = pl.ds(TILE, ny - 2 * TILE)
                rows = flat[orb, pl.ds((x + 2) * pitch + TILE, ny - 2 * TILE), :]
                packed[orb, group, there, :] = pack_z_lanes(
                    rows, plane, packed[orb, group, there, :]
                )


def edges(field, packed, nx, ny, halos, edge, last):
    orbs, nz = field.shape[0], field.shape[-1]
    args = [field, *halos] + ([] if last else [packed])
    shapes = [vmem_out(field.shape)]
    if not last:
        shapes += [vmem_out((orbs, 2, ny, nz))] * 2 + [vmem_out((orbs, 2, nx, nz))] * 2
        shapes += [vmem_out(packed.shape)]
    return pl.pallas_call(
        functools.partial(edges_kernel, nx, ny, edge, last),
        out_shape=tuple(shapes),
        in_specs=[WHOLE] * len(args),
        out_specs=(WHOLE,) * len(shapes),
        input_output_aliases={0: 0} if last else {0: 0, 5: 5},
        compiler_params=params(),
        cost_estimate=LITTLE,
        name="edges",
    )(*[in_vmem(arg) for arg in args])


def pair_list(orbs):
    return [(line, column) for line in range(orbs) for column in range(line, orbs)]


def gram_kernel(nx, ny, field, out):
    orbs = field.shape[0]
    pitch = ny + PAD
    flat = field.reshape(orbs, (nx + 4) * pitch, LANES)
    pairs = pair_list(orbs)

    def plane(x, totals):
        totals = list(totals)
        for tile in range(ny // TILE):
            start = pl.multiple_of((x + 2) * pitch + tile * TILE, TILE)
            rows = [flat[orb, pl.ds(start, TILE), :] for orb in range(orbs)]
            for index, (line, column) in enumerate(pairs):
                totals[index] = totals[index] + rows[line] * rows[column]
        return tuple(totals)

    zero = jnp.zeros((TILE, LANES), jnp.float32)
    totals = lax.fori_loop(0, nx, plane, (zero,) * len(pairs))
    out[...] = jnp.zeros_like(out)
    for index, total in enumerate(totals):
        out[pl.ds(index, 1), :] = jnp.sum(total, axis=0, keepdims=True)


def gram(field, nx, ny):
    orbs = field.shape[0]
    rows = -(-len(pair_list(orbs)) // TILE) * TILE
    return pl.pallas_call(
        functools.partial(gram_kernel, nx, ny),
        out_shape=jax.ShapeDtypeStruct((rows, LANES), jnp.float32),
        in_specs=[WHOLE],
        out_specs=WHOLE,
        compiler_params=params(),
        cost_estimate=LITTLE,
        name="gram",
    )(in_vmem(field))


def basis_kernel(nx, ny, chunk, cells, parts, field, *rest):
    sums, (out, factor, held, sems) = rest[:parts], rest[parts:]
    orbs = field.shape[0]
    pitch = ny + PAD
    flat = field.reshape(orbs, (nx + 4) * pitch, LANES)
    pairs = pair_list(orbs)

    total = sums[0][...]
    for part in sums[1:]:
        total = total + part[...]
    total = jnp.broadcast_to(jnp.sum(total, axis=1, keepdims=True), total.shape) / cells
    entry = {}
    for index, pair in enumerate(pairs):
        entry[pair] = total[index : index + 1, :]
    upper, inv = {}, {}
    for line in range(orbs):
        for column in range(line, orbs):
            value = entry[line, column]
            for inner in range(line):
                value = value - upper[inner, line] * upper[inner, column]
            if column == line:
                upper[line, line] = jnp.sqrt(value)
                inv[line, line] = 1.0 / upper[line, line]
            else:
                upper[line, column] = value * inv[line, line]
    for column in range(orbs):
        for line in range(column - 1, -1, -1):
            value = upper[line, line + 1] * inv[line + 1, column]
            for inner in range(line + 2, column + 1):
                value = value + upper[line, inner] * inv[inner, column]
            inv[line, column] = -value * inv[line, line]
    row = lax.broadcasted_iota(jnp.int32, (TILE, LANES), 0)
    col = lax.broadcasted_iota(jnp.int32, (TILE, LANES), 1)
    whole = jnp.zeros((TILE, LANES), jnp.float32)
    for (line, column), value in upper.items():
        there = (row == line) & (col == column)
        whole = jnp.where(there, jnp.broadcast_to(value, whole.shape), whole)
    factor[...] = whole[:orbs, :orbs]
    gains = {pair: jnp.broadcast_to(inv[pair], (TILE, LANES)) for pair in pairs}

    half = ny // TILE // 2
    pieces = [(plane, part) for plane in range(chunk) for part in (0, half)]

    def copy(index):
        place = pl.ds(index * chunk, chunk)
        return pltpu.make_async_copy(held.at[:, place], out.at[:, place], sems.at[index])

    @pl.loop(0, nx // chunk)
    def _(index):
        first = index * chunk

        def fetch(plane, part):
            rows = []
            for tile in range(part, part + half):
                start = pl.multiple_of((first + plane + 2) * pitch + tile * TILE, TILE)
                rows.append([flat[orb, pl.ds(start, TILE), :] for orb in range(orbs)])
            return rows

        rows = fetch(*pieces[0])
        for number, (plane, part) in enumerate(pieces):
            later = fetch(*pieces[number + 1]) if number + 1 < len(pieces) else None
            values = []
            for tile in range(half):
                for column in range(orbs):
                    value = rows[tile][0] * gains[0, column]
                    for line in range(1, column + 1):
                        value = value + rows[tile][line] * gains[line, column]
                    values.append(value)
            for tile in range(half):
                for column in range(orbs):
                    there = pl.ds((part + tile) * TILE, TILE)
                    held[column, first + plane, there, :] = values[tile * orbs + column]
            rows = later
        copy(index).start()

    @pl.loop(0, nx // chunk)
    def _(index):
        copy(index).wait()


def basis(field, nx, ny, sums, cells):
    orbs, nz = field.shape[0], field.shape[-1]
    chunk = 4
    return pl.pallas_call(
        functools.partial(basis_kernel, nx, ny, chunk, cells, len(sums)),
        out_shape=(
            jax.ShapeDtypeStruct((orbs, nx, ny, nz), jnp.float32),
            jax.ShapeDtypeStruct((orbs, orbs), jnp.float32),
        ),
        in_specs=[WHOLE] * (1 + len(sums)),
        out_specs=(pl.BlockSpec(memory_space=pltpu.HBM), WHOLE),
        scratch_shapes=[
            pltpu.VMEM((orbs, nx, ny, nz), jnp.float32),
            pltpu.SemaphoreType.DMA((nx // chunk,)),
        ],
        compiler_params=pltpu.CompilerParams(vmem_limit_bytes=VMEM_LIMIT + 4 * orbs * nx * ny * nz),
        cost_estimate=LITTLE,
        name="basis",
    )(in_vmem(field), *sums)


def exchanges(array, axis):
    count = lax.axis_size(axis)
    if count & (count - 1):
        moves = [[(i, (i + by) % count) for i in range(count)] for by in range(1, count)]
    else:
        moves = [[(i, i ^ by) for i in range(count)] for by in range(1, count)]
    return [lax.ppermute(array, axis, move) for move in moves]


def body(orbitals, potential):
    _, nx, ny, _ = orbitals.shape
    cells = (
        nx
        * lax.axis_size("gx")
        * (ny * lax.axis_size("gy"))
        * (orbitals.shape[3] * lax.axis_size("gz"))
    )
    orbitals = pltpu.with_memory_space_constraint(orbitals, pltpu.HBM)
    potential = pltpu.with_memory_space_constraint(potential, pltpu.HBM)
    x_faces = faces_x(orbitals)
    x_faces, orbitals = lax.optimization_barrier((x_faces, orbitals))
    field, weight, *y_faces, packed = load(orbitals, potential)
    before = None
    for level in range(3):
        last = level == 2
        halo_x = [swap(face, "gx", parity) for parity, face in enumerate(x_faces)]
        halo_y = [swap(face, "gy", parity) for parity, face in enumerate(y_faces)]
        z_even, z_odd = swap(packed, "gz", 0), swap(packed, "gz", 1)
        after, *packed = step(field, weight, z_even, z_odd, before, last)
        packed = None if last else packed[0]
        edge = EDGE * (0.5 if level == 0 else 1.0)
        after, *faces = edges(after, packed, nx, ny, (*halo_x, *halo_y), edge, last)
        if not last:
            x_faces, y_faces, packed = faces[:2], faces[2:4], faces[4]
        before, field = field, after
    local = gram(field, nx, ny)
    for axis in ("gz", "gy"):
        for part in exchanges(local, axis):
            local = local + part
    return basis(field, nx, ny, [local, *exchanges(local, "gx")], cells)


def solution(mesh):
    return jax.shard_map(
        body,
        mesh=mesh,
        in_specs=(P(None, "gx", "gy", "gz"), P("gx", "gy", "gz")),
        out_specs=(P(None, "gx", "gy", "gz"), P()),
        check_vma=False,
    )
```

```python
import functools

import jax
import jax.numpy as jnp
from jax import lax
from jax.experimental import pallas as pl
from jax.experimental.pallas import tpu as pltpu
from jax.sharding import PartitionSpec as P

CENTRE = 4.5
HALF_WIDTH = 3.5
EDGE = 2.0 / HALF_WIDTH / 24.0
BACK = (None, 2.0 / EDGE**2, 1.0 / EDGE**2)
FINAL = 0.5 * EDGE**3
LANES = 128
TILE = 8
PAD = 8
PER = LANES // 4
VMEM_LIMIT = 8 * 1024 * 1024


def vmem_out(shape):
    return pltpu.VMEM(shape, jnp.float32)


def in_vmem(array):
    return pltpu.with_memory_space_constraint(array, pltpu.VMEM)


WHOLE = pl.BlockSpec(memory_space=pltpu.VMEM)
ANYWHERE = pl.BlockSpec(memory_space=pl.ANY)


def params():
    return pltpu.CompilerParams(vmem_limit_bytes=VMEM_LIMIT)


LITTLE = pl.CostEstimate(flops=1, bytes_accessed=1, transcendentals=0)


def pairing(axis, parity):
    pairs = []
    for low in range(parity, lax.axis_size(axis) - 1, 2):
        pairs += [(low, low + 1), (low + 1, low)]
    return pairs


def swap(array, axis, parity):
    pairs = pairing(axis, parity)
    if not pairs:
        return jnp.zeros_like(array)
    return lax.ppermute(array, axis, pairs)


def is_odd(axis):
    return lax.rem(lax.axis_index(axis), 2) == 1


def pack_y_group(rows, even, odd, orb, group, flip):
    place = pl.ds(group * TILE, TILE)
    for layer in range(2):
        low, high = rows[layer], rows[2 + layer]
        even[orb, layer, place, :] = jnp.where(flip, low, high)
        odd[orb, layer, place, :] = jnp.where(flip, high, low)


def pack_z_lanes(rows, plane, total):
    lane = lax.broadcasted_iota(jnp.int32, rows.shape, 1)
    moved = pltpu.roll(rows, (4 * plane + 2) % LANES, 1)
    return moved if total is None else jnp.where(lane // 4 == plane, moved, total)


def pack_z_tiles(flat, packed, pitch, orb, group, tiles):
    totals = [None] * len(tiles)
    for plane in range(PER):
        for number, tile in enumerate(tiles):
            start = pl.multiple_of((group * PER + plane + 2) * pitch + tile * TILE, TILE)
            rows = flat[orb, pl.ds(start, TILE), :]
            totals[number] = pack_z_lanes(rows, plane, totals[number])
    for number, tile in enumerate(tiles):
        packed[orb, group, pl.ds(tile * TILE, TILE), :] = totals[number]


def pack_x(flat, even, odd, pitch, nx, ny, orb, flip):
    for layer in range(2):
        low = flat[orb, pl.ds((2 + layer) * pitch, ny), :]
        high = flat[orb, pl.ds((nx + layer) * pitch, ny), :]
        even[orb, layer] = jnp.where(flip, low, high)
        odd[orb, layer] = jnp.where(flip, high, low)


def load_kernel(
    nx, ny, field, potential, out, weight, x_even, x_odd, y_even, y_odd, packed, sems
):
    orbs = field.shape[0]
    pitch = ny + PAD
    groups = nx // PER
    flat = out.reshape(orbs, (nx + 4) * pitch, LANES)

    def copy(orb, group):
        return pltpu.make_async_copy(
            field.at[orb, pl.ds(group * PER, PER)],
            out.at[orb, pl.ds(2 + group * PER, PER), pl.ds(0, ny)],
            sems.at[orb * groups + group],
        )

    first = pltpu.make_async_copy(potential, weight, sems.at[orbs * groups])
    first.start()
    for orb in range(orbs):
        for group in range(groups):
            copy(orb, group).start()
    flip_x, flip_y = is_odd("gx"), is_odd("gy")
    zero_planes = jnp.zeros((2 * pitch, LANES), jnp.float32)
    zero_rows = jnp.zeros((PAD, LANES), jnp.float32)
    for orb in range(orbs):
        flat[orb, pl.ds(0, 2 * pitch), :] = zero_planes
        flat[orb, pl.ds((nx + 2) * pitch, 2 * pitch), :] = zero_planes

        @pl.loop(0, nx, unroll=8)
        def _(x):
            flat[orb, pl.ds(pl.multiple_of((x + 2) * pitch + ny, TILE), PAD), :] = zero_rows

    first.wait()

    @pl.loop(0, nx, unroll=2)
    def _(x):
        weight[x] = 24.0 * weight[x] + 24.0 * (0.5 * 7.5 - CENTRE)

    @pl.loop(0, orbs * groups)
    def _(index):
        orb, group = index // groups, lax.rem(index, groups)
        copy(orb, group).wait()
        pack_z_tiles(flat, packed, pitch, orb, group, range(ny // TILE))
        for part in range(PER // TILE):
            place = group * (PER // TILE) + part
            start = (place * TILE + 2) * pitch
            rows = [
                flat[orb, pl.ds(start + y, TILE, stride=pitch), :] for y in (0, 1, ny - 2, ny - 1)
            ]
            pack_y_group(rows, y_even, y_odd, orb, place, flip_y)

    @pl.loop(0, orbs)
    def _(orb):
        pack_x(flat, x_even, x_odd, pitch, nx, ny, orb, flip_x)


def load(orbitals, potential):
    orbs, nx, ny, nz = orbitals.shape
    return pl.pallas_call(
        functools.partial(load_kernel, nx, ny),
        out_shape=(
            vmem_out((orbs, nx + 4, ny + PAD, nz)),
            vmem_out((nx, ny, nz)),
            *[vmem_out((orbs, 2, ny, nz))] * 2,
            *[vmem_out((orbs, 2, nx, nz))] * 2,
            vmem_out((orbs, nx // PER, ny, nz)),
        ),
        in_specs=[ANYWHERE, ANYWHERE],
        out_specs=(WHOLE,) * 7,
        scratch_shapes=[pltpu.SemaphoreType.DMA((orbs * (nx // PER) + 1,))],
        compiler_params=params(),
        cost_estimate=LITTLE,
        name="load",
    )(orbitals, potential)


def store_late(ref, works):
    waiting = []
    for work, *where in works:
        ready = work(*where)
        for there, value in waiting:
            ref[there] = value
        waiting = ready
    for there, value in waiting:
        ref[there] = value


def step_kernel(nx, ny, back, last, field, weight, z_even, z_odd, *rest):
    first = back is None
    rest = rest if first else rest[1:]
    out, packed = rest[0], None if last else rest[1]
    correction, mix = rest[-2:]
    orbs = field.shape[0]
    pitch = ny + PAD
    flat = field.reshape(orbs, (nx + 4) * pitch, LANES)
    flat_out = out.reshape(orbs, (nx + 4) * pitch, LANES)
    groups = nx // PER
    tiles = ny // TILE
    flip = is_odd("gz")
    place = lax.broadcasted_iota(jnp.int32, (ny, LANES), 1) % 4
    lane = lax.broadcasted_iota(jnp.int32, (TILE, LANES), 1)
    ends = (lane < 2) | (lane >= LANES - 2)

    if first:
        zero_planes = jnp.zeros((2 * pitch, LANES), jnp.float32)
        zero_rows = jnp.zeros((PAD, LANES), jnp.float32)
        for orb in range(orbs):
            flat_out[orb, pl.ds(0, 2 * pitch), :] = zero_planes
            flat_out[orb, pl.ds((nx + 2) * pitch, 2 * pitch), :] = zero_planes

            @pl.loop(0, nx, unroll=8)
            def _(x):
                there = pl.ds(pl.multiple_of((x + 2) * pitch + ny, TILE), PAD)
                flat_out[orb, there, :] = zero_rows

    line = lax.broadcasted_iota(jnp.int32, (LANES, LANES), 0)
    column = lax.broadcasted_iota(jnp.int32, (LANES, LANES), 1)
    apart = jnp.abs(line - column)
    weights = jnp.where(apart == 1, -16.0, jnp.where(apart == 2, 1.0, 0.0)).astype(jnp.bfloat16)
    mix[pl.ds(0, LANES), :] = weights
    mix[pl.ds(LANES, LANES), :] = weights

    def add_beyond(orb, group):
        even, odd = z_even[orb, group], z_odd[orb, group]
        below = jnp.where(flip, even, odd)
        above = jnp.where(flip, odd, even)
        beyond = jnp.where(place < 2, below, above)
        left = pltpu.roll(beyond, LANES - 2, 1) - 16.0 * jnp.where(
            place == 1, pltpu.roll(beyond, LANES - 1, 1), 0.0
        )
        right = pltpu.roll(beyond, 2, 1) - 16.0 * jnp.where(
            place == 2, pltpu.roll(beyond, 1, 1), 0.0
        )
        return [((orb, group), jnp.where(place < 2, left, right))]

    store_late(correction, [(add_beyond, orb, group) for orb in range(orbs) for group in range(groups)])

    def locate(index, tile):
        orb, group = index // groups, lax.rem(index, groups)
        return orb, group, (group * PER + 2) * pitch + tile * TILE

    def along_z(index, tile):
        orb, group, base = locate(index, tile)
        rows = [
            flat[orb, pl.ds(pl.multiple_of(base + plane * pitch, TILE), TILE), :]
            for plane in range(PER)
        ]
        stacked = jnp.concatenate(rows, axis=0)
        high = stacked.astype(jnp.bfloat16)
        low = (stacked - high.astype(jnp.float32)).astype(jnp.bfloat16)
        product = jnp.dot(
            jnp.concatenate([high, low], axis=1), mix[...], preferred_element_type=jnp.float32
        )
        fix = correction[orb, group, pl.ds(tile * TILE, TILE), :]
        sums = []
        for plane in range(PER):
            moved = pltpu.roll(fix, LANES - 4 * plane - 2, 1)
            sums.append(
                product[plane * TILE : (plane + 1) * TILE] + jnp.where(ends, moved, 0.0)
            )
        return tuple(sums)

    def block(index, sums):
        for tile in range(tiles):
            if tile + 1 < tiles:
                later = along_z(index, tile + 1)
            else:
                later = along_z(jnp.minimum(index + 1, orbs * groups - 1), 0)
            finish(index, tile, sums)
            sums = later
        return sums

    def finish(index, tile, sums):
        orb, group, base = locate(index, tile)

        def rows(plane, shift=0):
            start = base + plane * pitch + shift
            if shift == 0:
                start = pl.multiple_of(start, TILE)
            return flat[orb, pl.ds(start, TILE), :]

        inner = not last and 0 < tile < tiles - 1
        mine = [rows(plane) for plane in range(-2, PER + 2)]
        values = []
        total = None
        for plane in range(PER):
            near = (mine[plane + 1] + mine[plane + 3]) + (rows(plane, -1) + rows(plane, 1))
            far = (mine[plane] + mine[plane + 4]) + (rows(plane, -2) + rows(plane, 2))
            ours = weight[group * PER + plane, pl.ds(tile * TILE, TILE), :]
            value = ours * mine[plane + 2] + ((far - 16.0 * near) + sums[plane])
            if not first:
                start = pl.multiple_of(base + plane * pitch, TILE)
                value = value - back * flat_out[orb, pl.ds(start, TILE), :]
            if inner:
                total = pack_z_lanes(value, plane, total)
            values.append(value)
        for plane in range(PER):
            start = pl.multiple_of(base + plane * pitch, TILE)
            flat_out[orb, pl.ds(start, TILE), :] = values[plane]
        if inner:
            packed[orb, group, pl.ds(tile * TILE, TILE), :] = total

    lax.fori_loop(0, orbs * groups, block, along_z(0, 0))


def step(field, weight, z_even, z_odd, before, back, last):
    orbs = field.shape[0]
    nx, ny, nz = weight.shape
    first = before is None
    args = [field, weight, z_even, z_odd] + ([] if first else [before])
    shapes = [vmem_out(field.shape)] + ([] if last else [vmem_out(z_even.shape)])
    return pl.pallas_call(
        functools.partial(step_kernel, nx, ny, back, last),
        out_shape=tuple(shapes),
        in_specs=[WHOLE] * len(args),
        out_specs=(WHOLE,) * len(shapes),
        scratch_shapes=[
            pltpu.VMEM((orbs, nx // PER, ny, nz), jnp.float32),
            pltpu.VMEM((2 * nz, nz), jnp.bfloat16),
        ],
        input_output_aliases={} if first else {4: 0},
        compiler_params=params(),
        cost_estimate=LITTLE,
        name="step",
    )(*[in_vmem(arg) for arg in args])


def edges_kernel(nx, ny, last, field, x_even, y_odd, y_even, x_odd, extra, *rest):
    orbs = field.shape[0]
    pitch = ny + PAD
    if last:
        out, products = rest
    else:
        out, next_x_even, next_x_odd, next_y_even, next_y_odd, packed = rest
    flat = out.reshape(orbs, (nx + 4) * pitch, LANES)
    flip_x, flip_y = is_odd("gx"), is_odd("gy")

    tiles = ny // TILE

    def plane_rows(x):
        return pl.ds((x + 2) * pitch, ny)

    def fix_x(orb):
        def halves(layer):
            even, odd = x_even[orb, layer], x_odd[orb, layer]
            return jnp.where(flip_x, even, odd), jnp.where(flip_x, odd, even)

        low_far, high_near = halves(0)
        low_near, high_far = halves(1)
        adds = (
            low_far - 16.0 * low_near,
            low_near,
            high_near,
            high_far - 16.0 * high_near,
        )
        return [
            ((orb, plane_rows(x), slice(None)), flat[orb, plane_rows(x), :] + add)
            for x, add in zip((0, 1, nx - 2, nx - 1), adds)
        ]

    store_late(flat, [(fix_x, orb) for orb in range(orbs)])

    def fix_y(orb, group):
        place = pl.ds(group * TILE, TILE)

        def pick(layer):
            even, odd = y_even[orb, layer, place, :], y_odd[orb, layer, place, :]
            return jnp.where(flip_y, even, odd), jnp.where(flip_y, odd, even)

        low_far, high_near = pick(0)
        low_near, high_far = pick(1)
        adds = (
            low_far - 16.0 * low_near,
            low_near,
            high_near,
            high_far - 16.0 * high_near,
        )
        start = (group * TILE + 2) * pitch
        rows = []
        for y, add in zip((0, 1, ny - 2, ny - 1), adds):
            there = pl.ds(start + y, TILE, stride=pitch)
            rows.append((there, flat[orb, there, :] + add))
        return rows

    @pl.loop(0, orbs)
    def _(orb):
        groups = range(nx // TILE)
        for half in (groups[: len(groups) // 2], groups[len(groups) // 2 :]):
            rows = [fix_y(orb, group) for group in half]
            for group, values in zip(half, rows):
                for there, value in values:
                    flat[orb, there, :] = value
                if not last:
                    pack_y_group(
                        [value for _, value in values], next_y_even, next_y_odd, orb, group, flip_y
                    )

    if not last:
        for orb in range(orbs):
            pack_x(flat, next_x_even, next_x_odd, pitch, nx, ny, orb, flip_x)

        def border(orb, group):
            ends = (0, tiles - 1)
            totals = [None] * len(ends)
            for plane in range(PER):
                for number, tile in enumerate(ends):
                    start = (group * PER + plane + 2) * pitch + tile * TILE
                    rows = flat[orb, pl.ds(start, TILE), :]
                    totals[number] = pack_z_lanes(rows, plane, totals[number])
            return [
                ((orb, group, pl.ds(tile * TILE, TILE), slice(None)), total)
                for tile, total in zip(ends, totals)
            ]

        def planes(orb, group):
            there = pl.ds(TILE, ny - 2 * TILE)
            total = extra[orb, group, there, :]
            for x in sorted({0, 1, nx - 2, nx - 1}):
                if x // PER == group:
                    rows = flat[orb, pl.ds((x + 2) * pitch + TILE, ny - 2 * TILE), :]
                    total = pack_z_lanes(rows, x % PER, total)
            return [((orb, group, there, slice(None)), total)]

        store_late(
            packed,
            [
                (work, orb, group)
                for orb in range(orbs)
                for group in range(nx // PER)
                for work in (border, planes)
            ],
        )

    if last:
        inside, border = range(1, tiles - 1), (0, tiles - 1)
        totals = [jnp.zeros((TILE, LANES), jnp.float32) for _ in pair_list(orbs)]
        for start, stop, tiles in (
            (0, nx, border),
            (0, 2, inside),
            (nx - 2, nx, inside),
        ):
            totals = add_products(flat, pitch, start, stop, tiles, totals)
        for index, total in enumerate(totals):
            there = pl.ds(index, 1)
            products[there, :] = extra[there, :] + jnp.sum(total, axis=0, keepdims=True)
        unused = pl.ds(len(totals), products.shape[0] - len(totals))
        products[unused, :] = extra[unused, :]


def edges(field, extra, nx, ny, halos, last):
    orbs, nz = field.shape[0], field.shape[-1]
    args = [field, *halos, extra]
    shapes = [vmem_out(field.shape)]
    if not last:
        shapes += [vmem_out((orbs, 2, ny, nz))] * 2 + [vmem_out((orbs, 2, nx, nz))] * 2
    shapes += [vmem_out(extra.shape)]
    return pl.pallas_call(
        functools.partial(edges_kernel, nx, ny, last),
        out_shape=tuple(shapes),
        in_specs=[WHOLE] * len(args),
        out_specs=(WHOLE,) * len(shapes),
        input_output_aliases={0: 0} if last else {0: 0, 5: 5},
        compiler_params=params(),
        cost_estimate=LITTLE,
        name="edges",
    )(*[in_vmem(arg) for arg in args])


def pair_list(orbs):
    return [(line, column) for line in range(orbs) for column in range(line, orbs)]


def add_products(flat, pitch, first, stop, tiles, totals):
    orbs = flat.shape[0]

    def plane(x, totals):
        totals = list(totals)
        for tile in tiles:
            start = pl.multiple_of((x + 2) * pitch + tile * TILE, TILE)
            rows = [flat[orb, pl.ds(start, TILE), :] for orb in range(orbs)]
            for index, (line, column) in enumerate(pair_list(orbs)):
                totals[index] = totals[index] + rows[line] * rows[column]
        return tuple(totals)

    return list(lax.fori_loop(first, stop, plane, tuple(totals)))


def products_kernel(nx, ny, field, out):
    orbs = field.shape[0]
    pitch = ny + PAD
    flat = field.reshape(orbs, (nx + 4) * pitch, LANES)
    totals = [jnp.zeros((TILE, LANES), jnp.float32) for _ in pair_list(orbs)]
    totals = add_products(flat, pitch, 2, nx - 2, range(1, ny // TILE - 1), totals)
    out[...] = jnp.zeros_like(out)
    for index, total in enumerate(totals):
        out[pl.ds(index, 1), :] = jnp.sum(total, axis=0, keepdims=True)


def products_inside(field, nx, ny):
    orbs = field.shape[0]
    rows = -(-len(pair_list(orbs)) // TILE) * TILE
    return pl.pallas_call(
        functools.partial(products_kernel, nx, ny),
        out_shape=vmem_out((rows, LANES)),
        in_specs=[WHOLE],
        out_specs=WHOLE,
        compiler_params=params(),
        cost_estimate=LITTLE,
        name="products",
    )(in_vmem(field))


def basis_kernel(nx, ny, chunk, cells, parts, field, *rest):
    sums, (out, factor, held, sems) = rest[:parts], rest[parts:]
    orbs = field.shape[0]
    pitch = ny + PAD
    flat = field.reshape(orbs, (nx + 4) * pitch, LANES)
    pairs = pair_list(orbs)

    total = sums[0][...]
    for part in sums[1:]:
        total = total + part[...]
    total = jnp.broadcast_to(jnp.sum(total, axis=1, keepdims=True), total.shape)
    total = total * (FINAL * FINAL / cells)
    entry = {}
    for index, pair in enumerate(pairs):
        entry[pair] = total[index : index + 1, :]
    upper, inv = {}, {}
    for line in range(orbs):
        for column in range(line, orbs):
            value = entry[line, column]
            for inner in range(line):
                value = value - upper[inner, line] * upper[inner, column]
            if column == line:
                inv[line, line] = lax.rsqrt(value)
                upper[line, line] = value * inv[line, line]
            else:
                upper[line, column] = value * inv[line, line]
    for column in range(orbs):
        for line in range(column - 1, -1, -1):
            value = upper[line, line + 1] * inv[line + 1, column]
            for inner in range(line + 2, column + 1):
                value = value + upper[line, inner] * inv[inner, column]
            inv[line, column] = -value * inv[line, line]
    row = lax.broadcasted_iota(jnp.int32, (TILE, LANES), 0)
    col = lax.broadcasted_iota(jnp.int32, (TILE, LANES), 1)
    whole = jnp.zeros((TILE, LANES), jnp.float32)
    for (line, column), value in upper.items():
        there = (row == line) & (col == column)
        whole = jnp.where(there, jnp.broadcast_to(value, whole.shape), whole)
    factor[...] = whole[:orbs, :orbs]
    gains = {pair: jnp.broadcast_to(inv[pair] * FINAL, (TILE, LANES)) for pair in pairs}

    half = ny // TILE // 2
    pieces = [(plane, part) for plane in range(chunk) for part in (0, half)]

    def copy(index):
        place = pl.ds(index * chunk, chunk)
        return pltpu.make_async_copy(held.at[:, place], out.at[:, place], sems.at[index])

    @pl.loop(0, nx // chunk)
    def _(index):
        first = index * chunk

        def fetch(plane, part):
            rows = []
            for tile in range(part, part + half):
                start = pl.multiple_of((first + plane + 2) * pitch + tile * TILE, TILE)
                rows.append([flat[orb, pl.ds(start, TILE), :] for orb in range(orbs)])
            return rows

        rows = fetch(*pieces[0])
        for number, (plane, part) in enumerate(pieces):
            later = fetch(*pieces[number + 1]) if number + 1 < len(pieces) else None
            values = []
            for tile in range(half):
                for column in range(orbs):
                    value = rows[tile][0] * gains[0, column]
                    for line in range(1, column + 1):
                        value = value + rows[tile][line] * gains[line, column]
                    values.append(value)
            for tile in range(half):
                for column in range(orbs):
                    there = pl.ds((part + tile) * TILE, TILE)
                    held[column, first + plane, there, :] = values[tile * orbs + column]
            rows = later
        copy(index).start()

    @pl.loop(0, nx // chunk)
    def _(index):
        copy(index).wait()


def basis(field, nx, ny, sums, cells):
    orbs, nz = field.shape[0], field.shape[-1]
    chunk = 4
    return pl.pallas_call(
        functools.partial(basis_kernel, nx, ny, chunk, cells, len(sums)),
        out_shape=(
            jax.ShapeDtypeStruct((orbs, nx, ny, nz), jnp.float32),
            jax.ShapeDtypeStruct((orbs, orbs), jnp.float32),
        ),
        in_specs=[WHOLE] * (1 + len(sums)),
        out_specs=(pl.BlockSpec(memory_space=pltpu.HBM), WHOLE),
        scratch_shapes=[
            pltpu.VMEM((orbs, nx, ny, nz), jnp.float32),
            pltpu.SemaphoreType.DMA((nx // chunk,)),
        ],
        compiler_params=pltpu.CompilerParams(vmem_limit_bytes=VMEM_LIMIT + 4 * orbs * nx * ny * nz),
        cost_estimate=LITTLE,
        name="basis",
    )(in_vmem(field), *sums)


def exchanges(array, axis):
    count = lax.axis_size(axis)
    if count & (count - 1):
        moves = [[(i, (i + by) % count) for i in range(count)] for by in range(1, count)]
    else:
        moves = [[(i, i ^ by) for i in range(count)] for by in range(1, count)]
    return [lax.ppermute(array, axis, move) for move in moves]


def body(orbitals, potential):
    _, nx, ny, _ = orbitals.shape
    cells = (
        nx
        * lax.axis_size("gx")
        * (ny * lax.axis_size("gy"))
        * (orbitals.shape[3] * lax.axis_size("gz"))
    )
    orbitals = pltpu.with_memory_space_constraint(orbitals, pltpu.HBM)
    potential = pltpu.with_memory_space_constraint(potential, pltpu.HBM)
    field, weight, *faces, packed = load(orbitals, potential)
    before = None
    for level in range(3):
        last = level == 2
        halos = []
        for axis, (even, odd) in (("gx", faces[:2]), ("gy", faces[2:])):
            halos += [swap(odd, axis, 1), swap(even, axis, 0)]
        z_even, z_odd = swap(packed, "gz", 0), swap(packed, "gz", 1)
        after, *extra = step(field, weight, z_even, z_odd, before, BACK[level], last)
        extra = products_inside(after, nx, ny) if last else extra[0]
        after, *faces, packed = edges(after, extra, nx, ny, [halos[1], halos[2], halos[3], halos[0]], last)
        before, field = field, after
    local = packed
    for axis in ("gz", "gy"):
        for part in exchanges(local, axis):
            local = local + part
    return basis(field, nx, ny, [local, *exchanges(local, "gx")], cells)


def solution(mesh):
    return jax.shard_map(
        body,
        mesh=mesh,
        in_specs=(P(None, "gx", "gy", "gz"), P("gx", "gy", "gz")),
        out_specs=(P(None, "gx", "gy", "gz"), P()),
        check_vma=False,
    )
```

```python
import functools

import jax
import jax.numpy as jnp
from jax import lax
from jax.experimental import pallas as pl
from jax.experimental.pallas import tpu as pltpu
from jax.sharding import PartitionSpec as P

CENTRE = 4.5
HALF_WIDTH = 3.5
EDGE = 2.0 / HALF_WIDTH / 24.0
BACK = (None, 2.0 / EDGE**2, 1.0 / EDGE**2)
FINAL = 0.5 * EDGE**3
LANES = 128
TILE = 8
PAD = 8
PER = LANES // 4
BATCH = 8
VMEM_LIMIT = 8 * 1024 * 1024


def vmem_out(shape):
    return pltpu.VMEM(shape, jnp.float32)


def in_vmem(array):
    return pltpu.with_memory_space_constraint(array, pltpu.VMEM)


WHOLE = pl.BlockSpec(memory_space=pltpu.VMEM)
ANYWHERE = pl.BlockSpec(memory_space=pl.ANY)


def params():
    return pltpu.CompilerParams(vmem_limit_bytes=VMEM_LIMIT)


LITTLE = pl.CostEstimate(flops=1, bytes_accessed=1, transcendentals=0)


def pairing(axis, parity):
    pairs = []
    for low in range(parity, lax.axis_size(axis) - 1, 2):
        pairs += [(low, low + 1), (low + 1, low)]
    return pairs


def swap(array, axis, parity):
    pairs = pairing(axis, parity)
    if not pairs:
        return jnp.zeros_like(array)
    return lax.ppermute(array, axis, pairs)


def is_odd(axis):
    return lax.rem(lax.axis_index(axis), 2) == 1


def pack_y_group(rows, even, odd, orb, group, flip):
    place = pl.ds(group * TILE, TILE)
    for layer in range(2):
        low, high = rows[layer], rows[2 + layer]
        even[orb, layer, place, :] = jnp.where(flip, low, high)
        odd[orb, layer, place, :] = jnp.where(flip, high, low)


def pack_z_lanes(rows, plane, total):
    lane = lax.broadcasted_iota(jnp.int32, rows.shape, 1)
    moved = pltpu.roll(rows, (4 * plane + 2) % LANES, 1)
    return moved if total is None else jnp.where(lane // 4 == plane, moved, total)


class Packer:
    def __init__(self):
        self.parts = []
        self.plane = 0

    def add(self, rows):
        lane = lax.broadcasted_iota(jnp.int32, rows.shape, 1)
        part, width = pltpu.roll(rows, (4 * self.plane + 2) % LANES, 1), 4
        while self.parts and self.parts[-1][1] == width:
            part = jnp.where(lane % (2 * width) < width, self.parts.pop()[0], part)
            width *= 2
        self.parts.append((part, width))
        self.plane += 1

    def total(self):
        ((part, _),) = self.parts
        return part


def pack_z_tiles(flat, packed, pitch, orb, group, tiles):
    packers = [Packer() for _ in tiles]
    for plane in range(PER):
        for packer, tile in zip(packers, tiles):
            start = pl.multiple_of((group * PER + plane + 2) * pitch + tile * TILE, TILE)
            packer.add(flat[orb, pl.ds(start, TILE), :])
    for packer, tile in zip(packers, tiles):
        packed[orb, group, pl.ds(tile * TILE, TILE), :] = packer.total()


def pack_x(flat, even, odd, pitch, nx, ny, orb, flip):
    for layer in range(2):
        low = flat[orb, pl.ds((2 + layer) * pitch, ny), :]
        high = flat[orb, pl.ds((nx + layer) * pitch, ny), :]
        even[orb, layer] = jnp.where(flip, low, high)
        odd[orb, layer] = jnp.where(flip, high, low)


def load_kernel(
    nx, ny, field, potential, out, weight, x_even, x_odd, y_even, y_odd, packed, blank, mix, sems
):
    orbs = field.shape[0]
    pitch = ny + PAD
    groups = nx // PER
    flat = out.reshape(orbs, (nx + 4) * pitch, LANES)
    other = blank.reshape(orbs, (nx + 4) * pitch, LANES)

    def copy(orb, group):
        return pltpu.make_async_copy(
            field.at[orb, pl.ds(group * PER, PER)],
            out.at[orb, pl.ds(2 + group * PER, PER), pl.ds(0, ny)],
            sems.at[orb * groups + group],
        )

    first = pltpu.make_async_copy(potential, weight, sems.at[orbs * groups])
    first.start()
    for orb in range(orbs):
        for group in range(groups):
            copy(orb, group).start()
    flip_x, flip_y = is_odd("gx"), is_odd("gy")
    zero_planes = jnp.zeros((2 * pitch, LANES), jnp.float32)
    zero_rows = jnp.zeros((PAD, LANES), jnp.float32)
    for rows in (flat, other):
        for orb in range(orbs):
            rows[orb, pl.ds(0, 2 * pitch), :] = zero_planes
            rows[orb, pl.ds((nx + 2) * pitch, 2 * pitch), :] = zero_planes

            @pl.loop(0, nx, unroll=8)
            def _(x):
                rows[orb, pl.ds(pl.multiple_of((x + 2) * pitch + ny, TILE), PAD), :] = zero_rows

    line = lax.broadcasted_iota(jnp.int32, (LANES, LANES), 0)
    column = lax.broadcasted_iota(jnp.int32, (LANES, LANES), 1)
    apart = jnp.abs(line - column)
    weights = jnp.where(apart == 1, -16.0, jnp.where(apart == 2, 1.0, 0.0)).astype(jnp.bfloat16)
    mix[pl.ds(0, LANES), :] = weights
    mix[pl.ds(LANES, LANES), :] = weights

    first.wait()

    @pl.loop(0, nx, unroll=2)
    def _(x):
        weight[x] = 24.0 * weight[x] + 24.0 * (0.5 * 7.5 - CENTRE)

    @pl.loop(0, orbs * groups)
    def _(index):
        orb, group = index // groups, lax.rem(index, groups)
        copy(orb, group).wait()
        pack_z_tiles(flat, packed, pitch, orb, group, range(ny // TILE))
        for part in range(PER // TILE):
            place = group * (PER // TILE) + part
            start = (place * TILE + 2) * pitch
            rows = [
                flat[orb, pl.ds(start + y, TILE, stride=pitch), :] for y in (0, 1, ny - 2, ny - 1)
            ]
            pack_y_group(rows, y_even, y_odd, orb, place, flip_y)

    @pl.loop(0, orbs)
    def _(orb):
        pack_x(flat, x_even, x_odd, pitch, nx, ny, orb, flip_x)


def load(orbitals, potential):
    orbs, nx, ny, nz = orbitals.shape
    return pl.pallas_call(
        functools.partial(load_kernel, nx, ny),
        out_shape=(
            vmem_out((orbs, nx + 4, ny + PAD, nz)),
            vmem_out((nx, ny, nz)),
            *[vmem_out((orbs, 2, ny, nz))] * 2,
            *[vmem_out((orbs, 2, nx, nz))] * 2,
            vmem_out((orbs, nx // PER, ny, nz)),
            vmem_out((orbs, nx + 4, ny + PAD, nz)),
            pltpu.VMEM((2 * nz, nz), jnp.bfloat16),
        ),
        in_specs=[ANYWHERE, ANYWHERE],
        out_specs=(WHOLE,) * 9,
        scratch_shapes=[pltpu.SemaphoreType.DMA((orbs * (nx // PER) + 1,))],
        compiler_params=params(),
        cost_estimate=LITTLE,
        name="load",
    )(orbitals, potential)


def store_late(ref, works):
    waiting = []
    for work, *where in works:
        ready = work(*where)
        for there, value in waiting:
            ref[there] = value
        waiting = ready
    for there, value in waiting:
        ref[there] = value


def step_kernel(nx, ny, back, last, field, weight, mix, z_even, z_odd, before, out, *rest):
    first = back is None
    packed, correction = None if last else rest[0], rest[-1]
    orbs = field.shape[0]
    pitch = ny + PAD
    flat = field.reshape(orbs, (nx + 4) * pitch, LANES)
    flat_out = out.reshape(orbs, (nx + 4) * pitch, LANES)
    groups = nx // PER
    tiles = ny // TILE
    flip = is_odd("gz")
    place = lax.broadcasted_iota(jnp.int32, (ny, LANES), 1) % 4
    lane = lax.broadcasted_iota(jnp.int32, (TILE, LANES), 1)
    ends = (lane < 2) | (lane >= LANES - 2)

    def add_beyond(orb, group):
        even, odd = z_even[orb, group], z_odd[orb, group]
        below = jnp.where(flip, even, odd)
        above = jnp.where(flip, odd, even)
        beyond = jnp.where(place < 2, below, above)
        left = pltpu.roll(beyond, LANES - 2, 1) - 16.0 * jnp.where(
            place == 1, pltpu.roll(beyond, LANES - 1, 1), 0.0
        )
        right = pltpu.roll(beyond, 2, 1) - 16.0 * jnp.where(
            place == 2, pltpu.roll(beyond, 1, 1), 0.0
        )
        return [((orb, group), jnp.where(place < 2, left, right))]

    store_late(correction, [(add_beyond, orb, group) for orb in range(orbs) for group in range(groups)])

    def locate(index, tile):
        orb, group = index // groups, lax.rem(index, groups)
        return orb, group, (group * PER + 2) * pitch + tile * TILE

    def along_z(index, tile):
        orb, group, base = locate(index, tile)
        rows = [
            flat[orb, pl.ds(pl.multiple_of(base + plane * pitch, TILE), TILE), :]
            for plane in range(PER)
        ]
        stacked = jnp.concatenate(rows, axis=0)
        high = stacked.astype(jnp.bfloat16)
        low = (stacked - high.astype(jnp.float32)).astype(jnp.bfloat16)
        product = jnp.dot(
            jnp.concatenate([high, low], axis=1), mix[...], preferred_element_type=jnp.float32
        )
        fix = correction[orb, group, pl.ds(tile * TILE, TILE), :]
        sums = []
        for plane in range(PER):
            moved = pltpu.roll(fix, LANES - 4 * plane - 2, 1)
            sums.append(
                product[plane * TILE : (plane + 1) * TILE] + jnp.where(ends, moved, 0.0)
            )
        return tuple(sums)

    def block(index, sums):
        for tile in range(tiles):
            if tile + 1 < tiles:
                later = along_z(index, tile + 1)
            else:
                later = along_z(jnp.minimum(index + 1, orbs * groups - 1), 0)
            finish(index, tile, sums)
            sums = later
        return sums

    def finish(index, tile, sums):
        orb, group, base = locate(index, tile)

        def rows(plane, shift=0):
            start = base + plane * pitch + shift
            if shift == 0:
                start = pl.multiple_of(start, TILE)
            return flat[orb, pl.ds(start, TILE), :]

        inner = not last and 0 < tile < tiles - 1
        mine = {plane: rows(plane) for plane in range(-2, 2)}
        packer = Packer()

        def some(first_plane):
            values = []
            for plane in range(first_plane, first_plane + BATCH):
                mine[plane + 2] = rows(plane + 2)
                near = (mine[plane - 1] + mine[plane + 1]) + (rows(plane, -1) + rows(plane, 1))
                far = (mine[plane - 2] + mine[plane + 2]) + (rows(plane, -2) + rows(plane, 2))
                ours = weight[group * PER + plane, pl.ds(tile * TILE, TILE), :]
                value = ours * mine[plane] + ((far - 16.0 * near) + sums[plane])
                there = pl.ds(pl.multiple_of(base + plane * pitch, TILE), TILE)
                if not first:
                    value = value - back * flat_out[orb, there, :]
                if inner:
                    packer.add(value)
                values.append(((orb, there, slice(None)), value))
            return values

        store_late(flat_out, [(some, plane) for plane in range(0, PER, BATCH)])
        if inner:
            packed[orb, group, pl.ds(tile * TILE, TILE), :] = packer.total()

    lax.fori_loop(0, orbs * groups, block, along_z(0, 0))


def step(field, weight, mix, z_even, z_odd, before, back, last):
    orbs = field.shape[0]
    nx, ny, nz = weight.shape
    args = [field, weight, mix, z_even, z_odd, before]
    shapes = [vmem_out(field.shape)] + ([] if last else [vmem_out(z_even.shape)])
    return pl.pallas_call(
        functools.partial(step_kernel, nx, ny, back, last),
        out_shape=tuple(shapes),
        in_specs=[WHOLE] * len(args),
        out_specs=(WHOLE,) * len(shapes),
        scratch_shapes=[pltpu.VMEM((orbs, nx // PER, ny, nz), jnp.float32)],
        input_output_aliases={5: 0},
        compiler_params=params(),
        cost_estimate=LITTLE,
        name="step",
    )(*[in_vmem(arg) for arg in args])


def edges_kernel(nx, ny, last, field, x_even, y_odd, y_even, x_odd, extra, *rest):
    orbs = field.shape[0]
    pitch = ny + PAD
    if last:
        out, products = rest
    else:
        out, next_x_even, next_x_odd, next_y_even, next_y_odd, packed = rest
    flat = out.reshape(orbs, (nx + 4) * pitch, LANES)
    flip_x, flip_y = is_odd("gx"), is_odd("gy")

    tiles = ny // TILE

    def plane_rows(x):
        return pl.ds((x + 2) * pitch, ny)

    def fix_x(orb):
        def halves(layer):
            even, odd = x_even[orb, layer], x_odd[orb, layer]
            return jnp.where(flip_x, even, odd), jnp.where(flip_x, odd, even)

        low_far, high_near = halves(0)
        low_near, high_far = halves(1)
        adds = (
            low_far - 16.0 * low_near,
            low_near,
            high_near,
            high_far - 16.0 * high_near,
        )
        return [
            ((orb, plane_rows(x), slice(None)), flat[orb, plane_rows(x), :] + add)
            for x, add in zip((0, 1, nx - 2, nx - 1), adds)
        ]

    store_late(flat, [(fix_x, orb) for orb in range(orbs)])

    def fix_y(orb, group):
        place = pl.ds(group * TILE, TILE)

        def pick(layer):
            even, odd = y_even[orb, layer, place, :], y_odd[orb, layer, place, :]
            return jnp.where(flip_y, even, odd), jnp.where(flip_y, odd, even)

        low_far, high_near = pick(0)
        low_near, high_far = pick(1)
        adds = (
            low_far - 16.0 * low_near,
            low_near,
            high_near,
            high_far - 16.0 * high_near,
        )
        start = (group * TILE + 2) * pitch
        rows = []
        for y, add in zip((0, 1, ny - 2, ny - 1), adds):
            there = pl.ds(start + y, TILE, stride=pitch)
            rows.append((there, flat[orb, there, :] + add))
        return rows

    @pl.loop(0, orbs)
    def _(orb):
        groups = range(nx // TILE)
        for half in (groups[: len(groups) // 2], groups[len(groups) // 2 :]):
            rows = [fix_y(orb, group) for group in half]
            for group, values in zip(half, rows):
                for there, value in values:
                    flat[orb, there, :] = value
                if not last:
                    pack_y_group(
                        [value for _, value in values], next_y_even, next_y_odd, orb, group, flip_y
                    )

    if not last:
        for orb in range(orbs):
            pack_x(flat, next_x_even, next_x_odd, pitch, nx, ny, orb, flip_x)

        def border(orb, group):
            ends = (0, tiles - 1)
            packers = [Packer() for _ in ends]
            for plane in range(PER):
                for packer, tile in zip(packers, ends):
                    start = (group * PER + plane + 2) * pitch + tile * TILE
                    packer.add(flat[orb, pl.ds(start, TILE), :])
            return [
                ((orb, group, pl.ds(tile * TILE, TILE), slice(None)), packer.total())
                for packer, tile in zip(packers, ends)
            ]

        def planes(orb, group):
            there = pl.ds(TILE, ny - 2 * TILE)
            total = extra[orb, group, there, :]
            for x in sorted({0, 1, nx - 2, nx - 1}):
                if x // PER == group:
                    rows = flat[orb, pl.ds((x + 2) * pitch + TILE, ny - 2 * TILE), :]
                    total = pack_z_lanes(rows, x % PER, total)
            return [((orb, group, there, slice(None)), total)]

        store_late(
            packed,
            [
                (work, orb, group)
                for orb in range(orbs)
                for group in range(nx // PER)
                for work in (border, planes)
            ],
        )

    if last:
        inside, border = range(1, tiles - 1), (0, tiles - 1)
        totals = [jnp.zeros((TILE, LANES), jnp.float32) for _ in pair_list(orbs)]
        for start, stop, tiles in (
            (0, nx, border),
            (0, 2, inside),
            (nx - 2, nx, inside),
        ):
            totals = add_products(flat, pitch, start, stop, tiles, totals)
        for index, total in enumerate(totals):
            there = pl.ds(index, 1)
            products[there, :] = extra[there, :] + jnp.sum(total, axis=0, keepdims=True)
        unused = pl.ds(len(totals), products.shape[0] - len(totals))
        products[unused, :] = extra[unused, :]


def edges(field, extra, nx, ny, halos, last):
    orbs, nz = field.shape[0], field.shape[-1]
    args = [field, *halos, extra]
    shapes = [vmem_out(field.shape)]
    if not last:
        shapes += [vmem_out((orbs, 2, ny, nz))] * 2 + [vmem_out((orbs, 2, nx, nz))] * 2
    shapes += [vmem_out(extra.shape)]
    return pl.pallas_call(
        functools.partial(edges_kernel, nx, ny, last),
        out_shape=tuple(shapes),
        in_specs=[WHOLE] * len(args),
        out_specs=(WHOLE,) * len(shapes),
        input_output_aliases={0: 0} if last else {0: 0, 5: 5},
        compiler_params=params(),
        cost_estimate=LITTLE,
        name="edges",
    )(*[in_vmem(arg) for arg in args])


def pair_list(orbs):
    return [(line, column) for line in range(orbs) for column in range(line, orbs)]


def add_products(flat, pitch, first, stop, tiles, totals):
    orbs = flat.shape[0]

    def plane(x, totals):
        totals = list(totals)
        for tile in tiles:
            start = pl.multiple_of((x + 2) * pitch + tile * TILE, TILE)
            rows = [flat[orb, pl.ds(start, TILE), :] for orb in range(orbs)]
            for index, (line, column) in enumerate(pair_list(orbs)):
                totals[index] = totals[index] + rows[line] * rows[column]
        return tuple(totals)

    return list(lax.fori_loop(first, stop, plane, tuple(totals)))


def products_kernel(nx, ny, field, out):
    orbs = field.shape[0]
    pitch = ny + PAD
    flat = field.reshape(orbs, (nx + 4) * pitch, LANES)
    totals = [jnp.zeros((TILE, LANES), jnp.float32) for _ in pair_list(orbs)]
    totals = add_products(flat, pitch, 2, nx - 2, range(1, ny // TILE - 1), totals)
    out[...] = jnp.zeros_like(out)
    for index, total in enumerate(totals):
        out[pl.ds(index, 1), :] = jnp.sum(total, axis=0, keepdims=True)


def products_inside(field, nx, ny):
    orbs = field.shape[0]
    rows = -(-len(pair_list(orbs)) // TILE) * TILE
    return pl.pallas_call(
        functools.partial(products_kernel, nx, ny),
        out_shape=vmem_out((rows, LANES)),
        in_specs=[WHOLE],
        out_specs=WHOLE,
        compiler_params=params(),
        cost_estimate=LITTLE,
        name="products",
    )(in_vmem(field))


def basis_kernel(nx, ny, chunk, cells, parts, field, *rest):
    sums, (out, factor, held, sems) = rest[:parts], rest[parts:]
    orbs = field.shape[0]
    pitch = ny + PAD
    flat = field.reshape(orbs, (nx + 4) * pitch, LANES)
    pairs = pair_list(orbs)

    total = sums[0][...]
    for part in sums[1:]:
        total = total + part[...]
    total = jnp.broadcast_to(jnp.sum(total, axis=1, keepdims=True), total.shape)
    total = total * (FINAL * FINAL / cells)
    entry = {}
    for index, pair in enumerate(pairs):
        entry[pair] = total[index : index + 1, :]
    upper, inv = {}, {}
    for line in range(orbs):
        for column in range(line, orbs):
            value = entry[line, column]
            for inner in range(line):
                value = value - upper[inner, line] * upper[inner, column]
            if column == line:
                inv[line, line] = lax.rsqrt(value)
                upper[line, line] = value * inv[line, line]
            else:
                upper[line, column] = value * inv[line, line]
    for column in range(orbs):
        for line in range(column - 1, -1, -1):
            value = upper[line, line + 1] * inv[line + 1, column]
            for inner in range(line + 2, column + 1):
                value = value + upper[line, inner] * inv[inner, column]
            inv[line, column] = -value * inv[line, line]
    row = lax.broadcasted_iota(jnp.int32, (TILE, LANES), 0)
    col = lax.broadcasted_iota(jnp.int32, (TILE, LANES), 1)
    whole = jnp.zeros((TILE, LANES), jnp.float32)
    for (line, column), value in upper.items():
        there = (row == line) & (col == column)
        whole = jnp.where(there, jnp.broadcast_to(value, whole.shape), whole)
    factor[...] = whole[:orbs, :orbs]
    gains = {pair: jnp.broadcast_to(inv[pair] * FINAL, (TILE, LANES)) for pair in pairs}

    half = ny // TILE // 2
    pieces = [(plane, part) for plane in range(chunk) for part in (0, half)]

    def copy(index):
        place = pl.ds(index * chunk, chunk)
        return pltpu.make_async_copy(held.at[:, place], out.at[:, place], sems.at[index])

    @pl.loop(0, nx // chunk)
    def _(index):
        first = index * chunk

        def fetch(plane, part):
            rows = []
            for tile in range(part, part + half):
                start = pl.multiple_of((first + plane + 2) * pitch + tile * TILE, TILE)
                rows.append([flat[orb, pl.ds(start, TILE), :] for orb in range(orbs)])
            return rows

        rows = fetch(*pieces[0])
        for number, (plane, part) in enumerate(pieces):
            later = fetch(*pieces[number + 1]) if number + 1 < len(pieces) else None
            values = []
            for tile in range(half):
                for column in range(orbs):
                    value = rows[tile][0] * gains[0, column]
                    for line in range(1, column + 1):
                        value = value + rows[tile][line] * gains[line, column]
                    values.append(value)
            for tile in range(half):
                for column in range(orbs):
                    there = pl.ds((part + tile) * TILE, TILE)
                    held[column, first + plane, there, :] = values[tile * orbs + column]
            rows = later
        copy(index).start()

    @pl.loop(0, nx // chunk)
    def _(index):
        copy(index).wait()


def basis(field, nx, ny, sums, cells):
    orbs, nz = field.shape[0], field.shape[-1]
    chunk = 4
    return pl.pallas_call(
        functools.partial(basis_kernel, nx, ny, chunk, cells, len(sums)),
        out_shape=(
            jax.ShapeDtypeStruct((orbs, nx, ny, nz), jnp.float32),
            jax.ShapeDtypeStruct((orbs, orbs), jnp.float32),
        ),
        in_specs=[WHOLE] * (1 + len(sums)),
        out_specs=(pl.BlockSpec(memory_space=pltpu.HBM), WHOLE),
        scratch_shapes=[
            pltpu.VMEM((orbs, nx, ny, nz), jnp.float32),
            pltpu.SemaphoreType.DMA((nx // chunk,)),
        ],
        compiler_params=pltpu.CompilerParams(vmem_limit_bytes=VMEM_LIMIT + 4 * orbs * nx * ny * nz),
        cost_estimate=LITTLE,
        name="basis",
    )(in_vmem(field), *sums)


def exchanges(array, axis):
    count = lax.axis_size(axis)
    if count & (count - 1):
        moves = [[(i, (i + by) % count) for i in range(count)] for by in range(1, count)]
    else:
        moves = [[(i, i ^ by) for i in range(count)] for by in range(1, count)]
    return [lax.ppermute(array, axis, move) for move in moves]


def body(orbitals, potential):
    _, nx, ny, _ = orbitals.shape
    cells = (
        nx
        * lax.axis_size("gx")
        * (ny * lax.axis_size("gy"))
        * (orbitals.shape[3] * lax.axis_size("gz"))
    )
    orbitals = pltpu.with_memory_space_constraint(orbitals, pltpu.HBM)
    potential = pltpu.with_memory_space_constraint(potential, pltpu.HBM)
    field, weight, *faces, packed, before, mix = load(orbitals, potential)
    for level in range(3):
        last = level == 2
        halos = []
        for axis, (even, odd) in (("gx", faces[:2]), ("gy", faces[2:])):
            halos += [swap(odd, axis, 1), swap(even, axis, 0)]
        z_even, z_odd = swap(packed, "gz", 0), swap(packed, "gz", 1)
        after, *extra = step(field, weight, mix, z_even, z_odd, before, BACK[level], last)
        extra = products_inside(after, nx, ny) if last else extra[0]
        after, *faces, packed = edges(after, extra, nx, ny, [halos[1], halos[2], halos[3], halos[0]], last)
        before, field = field, after
    local = packed
    for axis in ("gz", "gy"):
        for part in exchanges(local, axis):
            local = local + part
    return basis(field, nx, ny, [local, *exchanges(local, "gx")], cells)


def solution(mesh):
    return jax.shard_map(
        body,
        mesh=mesh,
        in_specs=(P(None, "gx", "gy", "gz"), P("gx", "gy", "gz")),
        out_specs=(P(None, "gx", "gy", "gz"), P()),
        check_vma=False,
    )
```
